32 devices in a mesh: row: 4 (over y, x), col: 8 (over z, core).
Axes of the slice: x: 2, y: 2, z: 4, core: 2. Of those that a mesh axis runs over, the one named last changes fastest.
Arguments:
- matrix_band: bfloat16 [48, 16, 128, 128], P('col', 'row'), may hold values from -9 to 9, as said below
- pattern: int32 [48, 16], P('col', 'row'), may hold values 0 or 1
- filter_mask: int32 [48, 16], P('col', 'row'), may hold values 0 or 1
Outputs:
- sign_iterate: bfloat16 [48, 16, 128, 128], P('col', 'row')
The draws below stay inside these ranges and needn't reach their ends.
Inputs may be any that keep to these rules, and one draw needn't show every extreme that they name: `matrix_band`: the tile at offset 0 of every block row is symmetric.
All inputs are finite; a program needn't handle non-finite values. No bound on the sum of `pattern` or of `filter_mask` on one device may be relied on, other than what follows from the above.
Results may differ from the reference program's by a relative error of at most 0.0031.
Values may be sent and summed in bfloat16 or wider, within the bound.
A program may use at most 192 MiB of HBM per device.

```python
import math
import jax
import jax.numpy as jnp
from jax import lax

TILE = 128
W = 16
NB = 48


def draw_matrix_band(key, part):
    extent = (NB, W, TILE, TILE)
    values = jnp.clip(jax.random.normal(key, extent, jnp.float32), -6.0, 6.0)
    leading = values[:, 0]
    mirror = (leading + jnp.swapaxes(leading, -1, -2)) * 0.70710677
    values = values.at[:, 0].set(mirror)
    return values.astype(jnp.bfloat16)


def set_ends(array, stream_key, smallest, high):
    shape = array.shape
    spot = [jax.random.randint(jax.random.fold_in(stream_key, axis), (), 0, shape[axis]) for axis in range(len(shape))]
    array = array.at[tuple(spot)].set(smallest)
    longest = shape.index(max(shape))
    spot[longest] = (spot[longest] + 1) % shape[longest]
    return array.at[tuple(spot)].set(high)


def setup_inputs(seed: int = 0) -> dict:
    key_list = jax.random.split(jax.random.key(seed), 4)
    return {
        "matrix_band": draw_matrix_band(jax.random.fold_in(key_list[3], 71), 0),
        "pattern": set_ends((jax.random.randint(key_list[1], (NB, W), 0, 4) < 3).astype(jnp.int32), jax.random.fold_in(key_list[1], 1), 0, 1),
        "filter_mask": set_ends((jax.random.randint(key_list[2], (NB, W), 0, 8) < 7).astype(jnp.int32), jax.random.fold_in(key_list[2], 1), 0, 1),
    }


def whole_rows(upper_band):
    mirrored = [jnp.swapaxes(jnp.roll(upper_band[:, offset], offset, axis=0), -1, -2) for offset in range(W - 1, 0, -1)]
    return jnp.concatenate([jnp.stack(mirrored, axis=1), upper_band], axis=1)

def band_product(left_rows, right_rows):
    padding = jnp.zeros((NB, W - 1) + right_rows.shape[2:], right_rows.dtype)
    padded = jnp.concatenate([padding, right_rows], axis=1)

    def one_offset(offset):
        moved = jnp.roll(padded, -offset, axis=0)
        right_block = lax.dynamic_slice_in_dim(moved, W - 1 - offset, 2 * W - 1, 1)
        return jnp.einsum('iapq,iarq->ipr', left_rows, right_block, precision=lax.Precision.HIGHEST)
    return jnp.moveaxis(lax.map(one_offset, jnp.arange(W, dtype=jnp.int32)), 0, 1)

def reference(matrix_band, pattern, filter_mask):
    factor = 1.0 / math.sqrt((2 * W - 1) * TILE)
    masked = matrix_band * pattern[:, :, None, None].astype(jnp.bfloat16)
    matrix_rows = whole_rows(masked.astype(jnp.float32))
    square_sum = band_product(matrix_rows, matrix_rows)
    square = (filter_mask[:, :, None, None].astype(jnp.float32) * (factor * factor) * square_sum).astype(jnp.bfloat16)
    square = lax.optimization_barrier(square)
    cube = band_product(whole_rows(square.astype(jnp.float32)), matrix_rows)
    result = pattern[:, :, None, None].astype(jnp.float32) * 0.5 * (3.0 * masked.astype(jnp.float32) - cube)
    return result.astype(jnp.bfloat16)
```

```python
import functools
import math

import jax
import jax.numpy as jnp
from jax import lax
from jax.experimental import pallas as pl
from jax.experimental.pallas import tpu as pltpu
from jax.sharding import PartitionSpec as P

MESH = pl.DeviceIdType.MESH
SLOTS = 7


def plan(matrix_band):
    rows, width, tile = matrix_band.shape[0], matrix_band.shape[1], matrix_band.shape[2]
    return rows, width, tile, rows // 2


def gather_kernel(R, C, n, lw, T, band_ref, pat_ref, fm_ref, g_ref, x_ref, local_sem, recv, zsend, rsend, ssend, ):
    r = lax.axis_index("row")
    c = lax.axis_index("col")
    core = lax.rem(c, 2)
    half = n // 2
    sib = c + 1 - 2 * core
    right, left = lax.rem(c + 2, C), lax.rem(c + C - 2, C)
    third = lax.rem(c + C - 3 + 6 * core, C)
    others = [lax.rem(r + d, R) for d in range(1, R)]

    barrier = pltpu.get_barrier_semaphore()
    partners = [(r, sib), (r, right), (r, left), (r, third)] + [(o, c) for o in others]
    for p in partners:
        pl.semaphore_signal(barrier, inc=1, device_id=p, device_id_type=MESH)

    for h in range(half):
        for a in range(2):
            i = 2 * h + a
            for t in range(lw):
                m = pat_ref[i, t].astype(jnp.float32)
                tile = band_ref[i, t].astype(jnp.float32) * m
                x_ref[h, a, t * T:(t + 1) * T, :] = tile.astype(jnp.bfloat16)
            pos = lax.broadcasted_iota(jnp.int32, (16, 128), 0)
            mask = jnp.zeros((16, 128), jnp.float32)
            for t in range(lw):
                mask = jnp.where(pos == t, fm_ref[i, t].astype(jnp.float32), mask)
            x_ref[h, a, lw * T:lw * T + 16, :] = mask.astype(jnp.bfloat16)

    pl.semaphore_wait(barrier, len(partners))

    def remote(src, g, rr, send_sem, dev):
        return pltpu.make_async_remote_copy(
            src_ref=src, dst_ref=g_ref.at[g, rr], send_sem=send_sem,
            recv_sem=recv.at[g, rr], device_id=dev, device_id_type=MESH)

    def when(cond, fn):
        if cond is True:
            fn()
        else:
            pl.when(cond)(fn)

    def arrived(g, rr):
        pltpu.make_async_copy(g_ref.at[g, rr], g_ref.at[g, rr], recv.at[g, rr]).wait()

    def g5(h, rr):
        return 2 * h + rr * lw <= 15 - 6 * core

    def g6(h, rr):
        return 2 * h + rr * lw <= 3

    own = lambda h: x_ref.at[h]
    sends = []

    def start(cond, make, waiters):
        when(cond, lambda: make().start())
        sends.append((cond, make))

    for h in range(half):
        start(True, lambda h=h: remote(own(h), half + h, r, zsend.at[0, h], (r, right)), sends)
        start(g5(h, r), lambda h=h: remote(own(h), 5 * half + h, r, zsend.at[1, h], (r, left)), sends)
    for h in range(half):
        if h >= 1:
            start(core == 1, lambda h=h: remote(own(h), h, r, zsend.at[2, h], (r, third)), sends)
        if h <= 1:
            start((core == 0) & g6(h, r),
                  lambda h=h: remote(own(h), 6 * half + h, r, zsend.at[2, h], (r, third)), sends)
    for h in range(half):
        for d, o in enumerate(others):
            start(True, lambda h=h, d=d, o=o: remote(own(h), 3 * half + h, r, rsend.at[3, h, d], (o, c)), sends)
        start(True, lambda h=h: remote(own(h), (4 * core + 2 * (1 - core)) * half + h, r,
                                       ssend.at[1, h, r], (r, sib)), sends)
        pltpu.make_async_copy(own(h), g_ref.at[3 * half + h, r], local_sem.at[h]).start()

    def to_row(cond, q, g, h):
        for d, o in enumerate(others):
            start(cond, lambda d=d, o=o: remote(g_ref.at[g, r], g, r, rsend.at[q, h, d], (o, c)), sends)

    def to_sib(q, s, h, rr):
        g = s * half + h
        dst = (s - 1 + 2 * core) * half + h
        if s == 1:
            cond = True if h >= 1 else core == 1
        elif s == 3:
            cond = True
        else:
            low = (core == 0) & (2 * h + rr * lw <= 15)
            cond = low | ((core == 1) & (2 * h + rr * lw <= 3)) if h <= 1 else low
        start(cond, lambda: remote(g_ref.at[g, rr], dst, rr, ssend.at[q, h, rr], (r, sib)), sends)

    for h in range(half):
        arrived(half + h, r)
        to_row(True, 0, half + h, h)
        to_sib(0, 1, h, r)
        when(g5(h, r), lambda h=h: arrived(5 * half + h, r))
        to_row(g5(h, r), 1, 5 * half + h, h)
        to_sib(2, 5, h, r)
        for o in others:
            arrived(3 * half + h, o)
            to_sib(1, 3, h, o)
    for h in range(half):
        if h >= 1:
            when(core == 0, lambda h=h: arrived(h, r))
            to_row(core == 0, 2, h, h)
        if h <= 1:
            cond = (core == 1) & g6(h, r)
            when(cond, lambda h=h: arrived(6 * half + h, r))
            to_row(cond, 2, 6 * half + h, h)
    for h in range(half):
        for o in others:
            arrived(half + h, o)
            to_sib(0, 1, h, o)
            when(g5(h, o), lambda h=h, o=o: arrived(5 * half + h, o))
            to_sib(2, 5, h, o)
    for h in range(half):
        for o in others:
            if h >= 1:
                when(core == 0, lambda h=h, o=o: arrived(h, o))
            if h <= 1:
                when((core == 1) & g6(h, o), lambda h=h, o=o: arrived(6 * half + h, o))
    for h in range(half):
        for rr in range(R):
            arrived(2 * half + h, rr)
            when((core == 0) | (2 * h + rr * lw <= 15), lambda h=h, rr=rr: arrived(4 * half + h, rr))
            if h <= 1 and 2 * h + rr * lw <= 3:
                when(core == 0, lambda h=h, rr=rr: arrived(6 * half + h, rr))
            if h >= 1:
                when(core == 1, lambda h=h, rr=rr: arrived(h, rr))
    for cond, make in sends:
        when(cond, lambda make=make: make().wait_send())
    for h in range(half):
        pltpu.make_async_copy(own(h), g_ref.at[3 * half + h, r], local_sem.at[h]).wait()


def compute_kernel(R, n, lw, T, W, g_ref, pat_ref, out_ref, a_ref, p_ref, m_ref, acc_ref):
    r = lax.axis_index("row")
    S = 2 * T
    half = n // 2
    M = n * T
    NL = SLOTS * half - 2
    factor = 1.0 / math.sqrt((2 * W - 1) * T)
    scale = factor * factor
    mid = W // 2

    def up(L, e, a):
        return g_ref[L + 1, e // lw, a, (e % lw) * T:(e % lw + 1) * T, :]

    def mask_row(L, e, a):
        return g_ref[L + 1, e // lw, a, lw * T:lw * T + 16, :].astype(jnp.float32)[e % lw:e % lw + 1, :]

    zero = jnp.zeros((T, T), jnp.bfloat16)

    @pl.loop(0, NL + 2)
    def _(L):
        a_ref[L] = jnp.zeros((M, S), jnp.bfloat16)
        m_ref[L] = jnp.zeros((n, 8, S), jnp.float32)

    p_ref[0] = jnp.zeros((M, S), jnp.bfloat16)
    p_ref[NL + 1] = jnp.zeros((M, S), jnp.bfloat16)

    @pl.loop(0, half)
    def _(I):
        for a in range(2):
            i = pl.multiple_of((2 * I + a) * T, T)
            for e in range(W):
                col, b = (a + e) // 2, (a + e) % 2
                a_ref[1 + mid + I + col, pl.ds(i, T), b * T:(b + 1) * T] = up(mid + I, e, a)
                m_ref[1 + mid + I + col, 2 * I + a, 0:1, b * T:(b + 1) * T] = mask_row(mid + I, e, a)
            for e in range(1, W):
                back, b = (a - e) // 2, (a - e) % 2
                a_ref[1 + mid + I + back, pl.ds(i, T), b * T:(b + 1) * T] = up(mid + I + back, e, b).T
                m_ref[1 + mid + I + back, 2 * I + a, 0:1, b * T:(b + 1) * T] = mask_row(mid + I + back, e, b)

    def super_tile(L, D):
        e = 2 * D
        if D == W // 2:
            top = jnp.concatenate([zero, zero], axis=1)
            low = jnp.concatenate([up(L, W - 1, 1), zero], axis=1)
        else:
            top = jnp.concatenate([up(L, e, 0), up(L, e + 1, 0)], axis=1)
            low = jnp.concatenate([up(L, e - 1, 1), up(L, e, 1)], axis=1)
        return jnp.concatenate([top, low], axis=0)

    def column(src, K):
        mirror = up(K, 1, 0)
        diag = jnp.concatenate(
            [jnp.concatenate([up(K, 0, 0), mirror], axis=1),
             jnp.concatenate([mirror.T, up(K, 0, 1)], axis=1)], axis=0)
        acc_ref[...] = jnp.dot(src[K + 1], diag, preferred_element_type=jnp.float32)
        for q in range(W // 4):
            near, far = 2 * q + 1, 2 * q + 2

            @pl.when(K - near >= 0)
            def _():
                left = jnp.concatenate([src[K + 1 - far], src[K + 1 - near]], axis=1)
                right = jnp.concatenate(
                    [super_tile(jnp.maximum(K - far, 0), far), super_tile(K - near, near)], axis=0)
                acc_ref[...] += jnp.dot(left, right, preferred_element_type=jnp.float32)

            @pl.when(K + far < NL)
            def _():
                left = jnp.concatenate([src[K + 1 + near], src[K + 1 + far]], axis=1)
                right = jnp.concatenate([super_tile(K, near), super_tile(K, far)], axis=1)
                acc_ref[...] += lax.dot_general(
                    left, right, (((1,), (1,)), ((), ())), preferred_element_type=jnp.float32)

            @pl.when(K + far == NL)
            def _():
                acc_ref[...] += lax.dot_general(
                    src[K + 1 + near], super_tile(K, near), (((1,), (1,)), ((), ())),
                    preferred_element_type=jnp.float32)

    @pl.loop(0, NL)
    def _(K):
        column(a_ref, K)
        for i in range(n):
            keep = m_ref[K + 1, i, 0:1, :] * scale
            p_ref[K + 1, i * T:(i + 1) * T, :] = (
                keep * acc_ref[i * T:(i + 1) * T, :]).astype(jnp.bfloat16)

    start = mid + r * (lw // 2)
    for jj in range((lw + n) // 2):
        column(p_ref, start + jj)
        for b in range(2):
            for i in range(n):
                t = 2 * jj + b - i
                if 0 <= t < lw:
                    cube = acc_ref[i * T:(i + 1) * T, b * T:(b + 1) * T]
                    own = g_ref[3 * half + i // 2, r, i % 2, t * T:(t + 1) * T, :].astype(jnp.float32)
                    keep = pat_ref[i, t].astype(jnp.float32) * 0.5
                    out_ref[i, t] = (keep * (3.0 * own - cube)).astype(jnp.bfloat16)


def on_device(R, C, matrix_band, pattern, filter_mask):
    n, lw, T, half = plan(matrix_band)
    W = lw * R
    rs = lw * T + 16
    bf = jnp.bfloat16
    window = pl.pallas_call(
        functools.partial(gather_kernel, R, C, n, lw, T),
        out_shape=jax.ShapeDtypeStruct((SLOTS * half, R, 2, rs, T), bf),
        in_specs=[
            pl.BlockSpec(memory_space=pltpu.VMEM),
            pl.BlockSpec(memory_space=pltpu.SMEM),
            pl.BlockSpec(memory_space=pltpu.SMEM),
        ],
        out_specs=pl.BlockSpec(memory_space=pl.ANY),
        scratch_shapes=[
            pltpu.VMEM((half, 2, rs, T), bf),
            pltpu.SemaphoreType.DMA((half,)),
            pltpu.SemaphoreType.DMA((SLOTS * half, R)),
            pltpu.SemaphoreType.DMA((3, half)),
            pltpu.SemaphoreType.DMA((4, half, R - 1)),
            pltpu.SemaphoreType.DMA((3, half, R)),
        ],
        compiler_params=pltpu.CompilerParams(
            collective_id=0, has_side_effects=True, vmem_limit_bytes=16 * 2**20),
    )(matrix_band, pattern, filter_mask)
    NL = SLOTS * half - 2
    return pl.pallas_call(
        functools.partial(compute_kernel, R, n, lw, T, W),
        out_shape=jax.ShapeDtypeStruct(matrix_band.shape, bf),
        in_specs=[
            pl.BlockSpec(memory_space=pltpu.VMEM),
            pl.BlockSpec(memory_space=pltpu.SMEM),
        ],
        out_specs=pl.BlockSpec(memory_space=pltpu.VMEM),
        scratch_shapes=[
            pltpu.VMEM((NL + 2, n * T, 2 * T), bf),
            pltpu.VMEM((NL + 2, n * T, 2 * T), bf),
            pltpu.VMEM((NL + 2, n, 8, 2 * T), jnp.float32),
            pltpu.VMEM((n * T, 2 * T), jnp.float32),
        ],
        compiler_params=pltpu.CompilerParams(vmem_limit_bytes=58 * 2**20),
    )(window, pattern)


def solution(mesh):
    placed = (P("col", "row", None, None), P("col", "row"), P("col", "row"))
    return jax.shard_map(
        functools.partial(on_device, mesh.shape["row"], mesh.shape["col"]),
        mesh=mesh,
        in_specs=placed,
        out_specs=P("col", "row", None, None),
        check_vma=False,
    )
```

```python
import functools
import math

import jax
import jax.numpy as jnp
from jax import lax
from jax.experimental import pallas as pl
from jax.experimental.pallas import tpu as pltpu
from jax.sharding import PartitionSpec as P

MESH = pl.DeviceIdType.MESH
SLOTS = 7
GROUP = 4
PAD = GROUP - 1


def plan(matrix_band):
    rows, width, tile = matrix_band.shape[0], matrix_band.shape[1], matrix_band.shape[2]
    return rows, width, tile, rows // 2


def gather_kernel(R, C, n, lw, T, band_ref, pat_ref, fm_ref, g_ref, x_ref, local_sem, recv, zsend, rsend, ssend, ):
    r = lax.axis_index("row")
    c = lax.axis_index("col")
    core = lax.rem(c, 2)
    half = n // 2
    sib = c + 1 - 2 * core
    right, left = lax.rem(c + 2, C), lax.rem(c + C - 2, C)
    third = lax.rem(c + C - 3 + 6 * core, C)
    if R == 4:
        side, over = r + 1 - 2 * lax.rem(r, 2), lax.rem(r + 2, 4)
        near, others = [side, over], [side, over, lax.rem(side + 2, 4)]
    else:
        others = near = [lax.rem(r + d, R) for d in range(1, R)]

    barrier = pltpu.get_barrier_semaphore()
    partners = [(r, sib), (r, right), (r, left), (r, third)] + [(o, c) for o in near]
    for p in partners:
        pl.semaphore_signal(barrier, inc=1, device_id=p, device_id_type=MESH)

    for h in range(half):
        for a in range(2):
            i = 2 * h + a
            for t in range(lw):
                m = pat_ref[i, t].astype(jnp.float32)
                tile = band_ref[i, t].astype(jnp.float32) * m
                x_ref[h, a, t * T:(t + 1) * T, :] = tile.astype(jnp.bfloat16)
            pos = lax.broadcasted_iota(jnp.int32, (16, 128), 0)
            mask = jnp.zeros((16, 128), jnp.float32)
            for t in range(lw):
                mask = jnp.where(pos == t, fm_ref[i, t].astype(jnp.float32), mask)
            x_ref[h, a, lw * T:lw * T + 16, :] = mask.astype(jnp.bfloat16)

    pl.semaphore_wait(barrier, len(partners))

    def remote(src, g, rr, send_sem, dev):
        return pltpu.make_async_remote_copy(
            src_ref=src, dst_ref=g_ref.at[g, rr], send_sem=send_sem,
            recv_sem=recv.at[g, rr], device_id=dev, device_id_type=MESH)

    def when(cond, fn):
        if cond is True:
            fn()
        else:
            pl.when(cond)(fn)

    def arrived(g, rr):
        pltpu.make_async_copy(g_ref.at[g, rr], g_ref.at[g, rr], recv.at[g, rr]).wait()

    def g5(h, rr):
        return 2 * h + rr * lw <= 15 - 6 * core

    def g6(h, rr):
        return 2 * h + rr * lw <= 3

    own = lambda h: x_ref.at[h]
    sends = []

    def start(cond, make, waiters):
        when(cond, lambda: make().start())
        sends.append((cond, make))

    for h in range(half):
        start(True, lambda h=h: remote(own(h), half + h, r, zsend.at[0, h], (r, right)), sends)
        start(g5(h, r), lambda h=h: remote(own(h), 5 * half + h, r, zsend.at[1, h], (r, left)), sends)
    for h in range(half):
        if h >= 1:
            start(core == 1, lambda h=h: remote(own(h), h, r, zsend.at[2, h], (r, third)), sends)
        if h <= 1:
            start((core == 0) & g6(h, r),
                  lambda h=h: remote(own(h), 6 * half + h, r, zsend.at[2, h], (r, third)), sends)
    for h in range(half):
        for d, o in enumerate(near):
            start(True, lambda h=h, d=d, o=o: remote(own(h), 3 * half + h, r, rsend.at[3, h, d], (o, c)), sends)
        start(True, lambda h=h: remote(own(h), (4 * core + 2 * (1 - core)) * half + h, r,
                                       ssend.at[1, h, r], (r, sib)), sends)
        pltpu.make_async_copy(own(h), g_ref.at[3 * half + h, r], local_sem.at[h]).start()

    def to_row(cond, q, g, h):
        for d, o in enumerate(near):
            start(cond, lambda d=d, o=o: remote(g_ref.at[g, r], g, r, rsend.at[q, h, d], (o, c)), sends)

    def to_sib(q, s, h, rr):
        g = s * half + h
        dst = (s - 1 + 2 * core) * half + h
        if s == 1:
            cond = True if h >= 1 else core == 1
        elif s == 3:
            cond = True
        else:
            low = (core == 0) & (2 * h + rr * lw <= 15)
            cond = low | ((core == 1) & (2 * h + rr * lw <= 3)) if h <= 1 else low
        start(cond, lambda: remote(g_ref.at[g, rr], dst, rr, ssend.at[q, h, rr], (r, sib)), sends)

    def to_diagonal(cond, q, s, h, index):
        if R != 4 or index != (s // 2 + h) % 2:
            return
        g, rr, dev = s * half + h, near[index], (near[1 - index], c)
        start(cond, lambda: remote(g_ref.at[g, rr], g, rr, rsend.at[q, h, 2], dev), sends)

    for h in range(half):
        arrived(half + h, r)
        to_row(True, 0, half + h, h)
        to_sib(0, 1, h, r)
        when(g5(h, r), lambda h=h: arrived(5 * half + h, r))
        to_row(g5(h, r), 1, 5 * half + h, h)
        to_sib(2, 5, h, r)
        for d, o in enumerate(others):
            arrived(3 * half + h, o)
            to_diagonal(True, 3, 3, h, d)
            to_sib(1, 3, h, o)
    for h in range(half):
        if h >= 1:
            when(core == 0, lambda h=h: arrived(h, r))
            to_row(core == 0, 2, h, h)
        if h <= 1:
            cond = (core == 1) & g6(h, r)
            when(cond, lambda h=h: arrived(6 * half + h, r))
            to_row(cond, 2, 6 * half + h, h)
    for h in range(half):
        for d, o in enumerate(others):
            arrived(half + h, o)
            to_diagonal(True, 0, 1, h, d)
            to_sib(0, 1, h, o)
            when(g5(h, o), lambda h=h, o=o: arrived(5 * half + h, o))
            to_diagonal(g5(h, o), 1, 5, h, d)
            to_sib(2, 5, h, o)
    for h in range(half):
        for d, o in enumerate(others):
            if h >= 1:
                when(core == 0, lambda h=h, o=o: arrived(h, o))
                to_diagonal(core == 0, 2, 0, h, d)
            if h <= 1:
                cond = (core == 1) & g6(h, o)
                when(cond, lambda h=h, o=o: arrived(6 * half + h, o))
                to_diagonal(cond, 2, 6, h, d)
    for h in range(half):
        for rr in range(R):
            arrived(2 * half + h, rr)
            when((core == 0) | (2 * h + rr * lw <= 15), lambda h=h, rr=rr: arrived(4 * half + h, rr))
            if h <= 1 and 2 * h + rr * lw <= 3:
                when(core == 0, lambda h=h, rr=rr: arrived(6 * half + h, rr))
            if h >= 1:
                when(core == 1, lambda h=h, rr=rr: arrived(h, rr))
    for cond, make in sends:
        when(cond, lambda make=make: make().wait_send())
    for h in range(half):
        pltpu.make_async_copy(own(h), g_ref.at[3 * half + h, r], local_sem.at[h]).wait()


def compute_kernel(R, n, lw, T, W, g_ref, pat_ref, out_ref, a_ref, p_ref, m_ref, acc_ref):
    r = lax.axis_index("row")
    S = 2 * T
    half = n // 2
    M = n * T
    NL = SLOTS * half - 2
    factor = 1.0 / math.sqrt((2 * W - 1) * T)
    scale = factor * factor
    mid = W // 2

    def up(L, e, a):
        return g_ref[L + 1, e // lw, a, (e % lw) * T:(e % lw + 1) * T, :]

    def mask_row(L, e, a):
        return g_ref[L + 1, e // lw, a, lw * T:lw * T + 16, :].astype(jnp.float32)[e % lw:e % lw + 1, :]

    zero = jnp.zeros((T, T), jnp.bfloat16)

    @pl.loop(0, NL + 2 * PAD)
    def _(L):
        a_ref[L] = jnp.zeros((M, S), jnp.bfloat16)
        m_ref[L] = jnp.zeros((n, 8, S), jnp.float32)

    for pad in range(PAD):
        p_ref[pad] = jnp.zeros((M, S), jnp.bfloat16)
        p_ref[NL + PAD + pad] = jnp.zeros((M, S), jnp.bfloat16)

    @pl.loop(0, half)
    def _(I):
        for a in range(2):
            i = pl.multiple_of((2 * I + a) * T, T)
            for e in range(W):
                col, b = (a + e) // 2, (a + e) % 2
                a_ref[PAD + mid + I + col, pl.ds(i, T), b * T:(b + 1) * T] = up(mid + I, e, a)
                m_ref[PAD + mid + I + col, 2 * I + a, 0:1, b * T:(b + 1) * T] = mask_row(mid + I, e, a)
            for e in range(1, W):
                back, b = (a - e) // 2, (a - e) % 2
                a_ref[PAD + mid + I + back, pl.ds(i, T), b * T:(b + 1) * T] = up(mid + I + back, e, b).T
                m_ref[PAD + mid + I + back, 2 * I + a, 0:1, b * T:(b + 1) * T] = mask_row(mid + I + back, e, b)

    def super_tile(L, D):
        e = 2 * D
        if D == W // 2:
            top = jnp.concatenate([zero, zero], axis=1)
            low = jnp.concatenate([up(L, W - 1, 1), zero], axis=1)
        else:
            top = jnp.concatenate([up(L, e, 0), up(L, e + 1, 0)], axis=1)
            low = jnp.concatenate([up(L, e - 1, 1), up(L, e, 1)], axis=1)
        return jnp.concatenate([top, low], axis=0)

    def column(src, K, lo, hi):
        def left(*places):
            parts = [src[place, lo:hi, :] for place in places]
            return parts[0] if len(parts) == 1 else jnp.concatenate(parts, axis=1)

        def mirrored(*distances):
            parts = [super_tile(K, D) for D in distances]
            right = parts[0] if len(parts) == 1 else jnp.concatenate(parts, axis=1)
            acc_ref[lo:hi] += lax.dot_general(
                left(*[K + PAD + D for D in distances]), right, (((1,), (1,)), ((), ())),
                preferred_element_type=jnp.float32)

        mirror = up(K, 1, 0)
        diag = jnp.concatenate(
            [jnp.concatenate([up(K, 0, 0), mirror], axis=1),
             jnp.concatenate([mirror.T, up(K, 0, 1)], axis=1)], axis=0)
        acc_ref[lo:hi] = jnp.dot(left(K + PAD), diag, preferred_element_type=jnp.float32)
        for q in range(W // 2 // GROUP):
            steps = [q * GROUP + D for D in range(1, GROUP + 1)]

            @pl.when(K - steps[0] >= 0)
            def _():
                right = jnp.concatenate(
                    [super_tile(jnp.maximum(K - D, 0), D) for D in steps], axis=0)
                acc_ref[lo:hi] += jnp.dot(
                    left(*[K + PAD - D for D in steps]), right, preferred_element_type=jnp.float32)

            @pl.when(K + steps[-1] < NL)
            def _():
                mirrored(*steps)

            for D in steps[:-1]:
                @pl.when((K + D < NL) & (K + steps[-1] >= NL))
                def _(D=D):
                    mirrored(D)

    @pl.loop(0, NL)
    def _(K):
        column(a_ref, K, 0, M)
        for i in range(n):
            keep = m_ref[K + PAD, i, 0:1, :] * scale
            p_ref[K + PAD, i * T:(i + 1) * T, :] = (
                keep * acc_ref[i * T:(i + 1) * T, :]).astype(jnp.bfloat16)

    start = mid + r * (lw // 2)
    for jj in range((lw + n) // 2):
        low = max(0, 2 * jj - lw + 1) // 2 * 2
        high = min(n, 2 * jj + 2)
        column(p_ref, start + jj, low * T, high * T)
        for b in range(2):
            for i in range(n):
                t = 2 * jj + b - i
                if 0 <= t < lw:
                    cube = acc_ref[i * T:(i + 1) * T, b * T:(b + 1) * T]
                    own = g_ref[3 * half + i // 2, r, i % 2, t * T:(t + 1) * T, :].astype(jnp.float32)
                    keep = pat_ref[i, t].astype(jnp.float32) * 0.5
                    out_ref[i, t] = (keep * (3.0 * own - cube)).astype(jnp.bfloat16)


def on_device(R, C, matrix_band, pattern, filter_mask):
    n, lw, T, half = plan(matrix_band)
    W = lw * R
    rs = lw * T + 16
    bf = jnp.bfloat16
    window = pl.pallas_call(
        functools.partial(gather_kernel, R, C, n, lw, T),
        out_shape=jax.ShapeDtypeStruct((SLOTS * half, R, 2, rs, T), bf),
        in_specs=[
            pl.BlockSpec(memory_space=pltpu.VMEM),
            pl.BlockSpec(memory_space=pltpu.SMEM),
            pl.BlockSpec(memory_space=pltpu.SMEM),
        ],
        out_specs=pl.BlockSpec(memory_space=pl.ANY),
        scratch_shapes=[
            pltpu.VMEM((half, 2, rs, T), bf),
            pltpu.SemaphoreType.DMA((half,)),
            pltpu.SemaphoreType.DMA((SLOTS * half, R)),
            pltpu.SemaphoreType.DMA((3, half)),
            pltpu.SemaphoreType.DMA((4, half, R - 1)),
            pltpu.SemaphoreType.DMA((3, half, R)),
        ],
        compiler_params=pltpu.CompilerParams(
            collective_id=0, has_side_effects=True, vmem_limit_bytes=16 * 2**20),
    )(matrix_band, pattern, filter_mask)
    NL = SLOTS * half - 2
    return pl.pallas_call(
        functools.partial(compute_kernel, R, n, lw, T, W),
        out_shape=jax.ShapeDtypeStruct(matrix_band.shape, bf),
        in_specs=[
            pl.BlockSpec(memory_space=pltpu.VMEM),
            pl.BlockSpec(memory_space=pltpu.SMEM),
        ],
        out_specs=pl.BlockSpec(memory_space=pltpu.VMEM),
        scratch_shapes=[
            pltpu.VMEM((NL + 2 * PAD, n * T, 2 * T), bf),
            pltpu.VMEM((NL + 2 * PAD, n * T, 2 * T), bf),
            pltpu.VMEM((NL + 2 * PAD, n, 8, 2 * T), jnp.float32),
            pltpu.VMEM((n * T, 2 * T), jnp.float32),
        ],
        compiler_params=pltpu.CompilerParams(vmem_limit_bytes=58 * 2**20),
    )(window, pattern)


def solution(mesh):
    placed = (P("col", "row", None, None), P("col", "row"), P("col", "row"))
    return jax.shard_map(
        functools.partial(on_device, mesh.shape["row"], mesh.shape["col"]),
        mesh=mesh,
        in_specs=placed,
        out_specs=P("col", "row", None, None),
        check_vma=False,
    )
```

```python
import functools
import math

import jax
import jax.numpy as jnp
from jax import lax
from jax.experimental import pallas as pl
from jax.experimental.pallas import tpu as pltpu
from jax.sharding import PartitionSpec as P

MESH = pl.DeviceIdType.MESH
SLOTS = 7
GROUP = 4
PAD = GROUP - 1


def plan(matrix_band):
    rows, width, tile = matrix_band.shape[0], matrix_band.shape[1], matrix_band.shape[2]
    return rows, width, tile, rows // 2


def kernel(R, C, n, lw, T, W, band_ref, pat_ref, fm_ref, out_ref, g_ref, x_ref, a_ref, p_ref, m_ref, acc_ref,
           local_sem, recv, zsend, rsend, ssend):
    clear, left_panel, square_columns, cube = compute_steps(
        R, n, lw, T, W, g_ref, pat_ref, out_ref, a_ref, p_ref, m_ref, acc_ref)
    r = lax.axis_index("row")
    c = lax.axis_index("col")
    core = lax.rem(c, 2)
    half = n // 2
    sib = c + 1 - 2 * core
    right, left = lax.rem(c + 2, C), lax.rem(c + C - 2, C)
    third = lax.rem(c + C - 3 + 6 * core, C)
    if R == 4:
        side, over = r + 1 - 2 * lax.rem(r, 2), lax.rem(r + 2, 4)
        near, others = [side, over], [side, over, lax.rem(side + 2, 4)]
    else:
        others = near = [lax.rem(r + d, R) for d in range(1, R)]

    barrier = pltpu.get_barrier_semaphore()
    partners = [(r, sib), (r, right), (r, left), (r, third)] + [(o, c) for o in near]
    for p in partners:
        pl.semaphore_signal(barrier, inc=1, device_id=p, device_id_type=MESH)

    for h in range(half):
        for a in range(2):
            i = 2 * h + a
            for t in range(lw):
                m = pat_ref[i, t].astype(jnp.float32)
                tile = band_ref[i, t].astype(jnp.float32) * m
                x_ref[h, a, t * T:(t + 1) * T, :] = tile.astype(jnp.bfloat16)
            pos = lax.broadcasted_iota(jnp.int32, (16, 128), 0)
            mask = jnp.zeros((16, 128), jnp.float32)
            for t in range(lw):
                mask = jnp.where(pos == t, fm_ref[i, t].astype(jnp.float32), mask)
            x_ref[h, a, lw * T:lw * T + 16, :] = mask.astype(jnp.bfloat16)

    pl.semaphore_wait(barrier, len(partners))

    def remote(src, g, rr, send_sem, dev):
        return pltpu.make_async_remote_copy(
            src_ref=src, dst_ref=g_ref.at[g, rr], send_sem=send_sem,
            recv_sem=recv.at[g, rr], device_id=dev, device_id_type=MESH)

    def when(cond, fn):
        if cond is True:
            fn()
        else:
            pl.when(cond)(fn)

    def arrived(g, rr):
        pltpu.make_async_copy(g_ref.at[g, rr], g_ref.at[g, rr], recv.at[g, rr]).wait()

    def g5(h, rr):
        return 2 * h + rr * lw <= 15 - 6 * core

    def g6(h, rr):
        return 2 * h + rr * lw <= 3

    own = lambda h: x_ref.at[h]
    sends = []

    def start(cond, make, waiters):
        when(cond, lambda: make().start())
        sends.append((cond, make))

    for h in range(half):
        start(True, lambda h=h: remote(own(h), half + h, r, zsend.at[0, h], (r, right)), sends)
        start(g5(h, r), lambda h=h: remote(own(h), 5 * half + h, r, zsend.at[1, h], (r, left)), sends)
    for h in range(half):
        if h >= 1:
            start(core == 1, lambda h=h: remote(own(h), h, r, zsend.at[2, h], (r, third)), sends)
        if h <= 1:
            start((core == 0) & g6(h, r),
                  lambda h=h: remote(own(h), 6 * half + h, r, zsend.at[2, h], (r, third)), sends)
    for h in range(half):
        for d, o in enumerate(near):
            start(True, lambda h=h, d=d, o=o: remote(own(h), 3 * half + h, r, rsend.at[3, h, d], (o, c)), sends)
        start(True, lambda h=h: remote(own(h), (4 * core + 2 * (1 - core)) * half + h, r,
                                       ssend.at[1, h, r], (r, sib)), sends)
        pltpu.make_async_copy(own(h), g_ref.at[3 * half + h, r], local_sem.at[h]).start()

    def to_row(cond, q, g, h):
        for d, o in enumerate(near):
            start(cond, lambda d=d, o=o: remote(g_ref.at[g, r], g, r, rsend.at[q, h, d], (o, c)), sends)

    def to_sib(q, s, h, rr):
        g = s * half + h
        dst = (s - 1 + 2 * core) * half + h
        if s == 1:
            cond = True if h >= 1 else core == 1
        elif s == 3:
            cond = True
        else:
            low = (core == 0) & (2 * h + rr * lw <= 15)
            cond = low | ((core == 1) & (2 * h + rr * lw <= 3)) if h <= 1 else low
        start(cond, lambda: remote(g_ref.at[g, rr], dst, rr, ssend.at[q, h, rr], (r, sib)), sends)

    def to_diagonal(cond, q, s, h, index):
        if R != 4 or index != (s // 2 + h) % 2:
            return
        g, rr, dev = s * half + h, near[index], (near[1 - index], c)
        start(cond, lambda: remote(g_ref.at[g, rr], g, rr, rsend.at[q, h, 2], dev), sends)

    clear()

    for h in range(half):
        arrived(half + h, r)
        to_row(True, 0, half + h, h)
        to_sib(0, 1, h, r)
        when(g5(h, r), lambda h=h: arrived(5 * half + h, r))
        to_row(g5(h, r), 1, 5 * half + h, h)
        to_sib(2, 5, h, r)
        for d, o in enumerate(others):
            arrived(3 * half + h, o)
            to_diagonal(True, 3, 3, h, d)
            to_sib(1, 3, h, o)
    for h in range(half):
        if h >= 1:
            when(core == 0, lambda h=h: arrived(h, r))
            to_row(core == 0, 2, h, h)
        if h <= 1:
            cond = (core == 1) & g6(h, r)
            when(cond, lambda h=h: arrived(6 * half + h, r))
            to_row(cond, 2, 6 * half + h, h)
    for h in range(half):
        for d, o in enumerate(others):
            arrived(half + h, o)
            to_diagonal(True, 0, 1, h, d)
            to_sib(0, 1, h, o)
            when(g5(h, o), lambda h=h, o=o: arrived(5 * half + h, o))
            to_diagonal(g5(h, o), 1, 5, h, d)
            to_sib(2, 5, h, o)
    for h in range(half):
        for d, o in enumerate(others):
            if h >= 1:
                when(core == 0, lambda h=h, o=o: arrived(h, o))
                to_diagonal(core == 0, 2, 0, h, d)
            if h <= 1:
                cond = (core == 1) & g6(h, o)
                when(cond, lambda h=h, o=o: arrived(6 * half + h, o))
                to_diagonal(cond, 2, 6, h, d)
    for h in range(half):
        for rr in range(R):
            arrived(2 * half + h, rr)
            if h >= 1:
                when(core == 1, lambda h=h, rr=rr: arrived(h, rr))
        pltpu.make_async_copy(own(h), g_ref.at[3 * half + h, r], local_sem.at[h]).wait()
    left_panel()
    first = 4 * half - 1
    square_columns(0, first)
    for h in range(half):
        for rr in range(R):
            when((core == 0) | (2 * h + rr * lw <= 15), lambda h=h, rr=rr: arrived(4 * half + h, rr))
            if h <= 1 and 2 * h + rr * lw <= 3:
                when(core == 0, lambda h=h, rr=rr: arrived(6 * half + h, rr))
    square_columns(first, SLOTS * half - 2)
    cube()
    for cond, make in sends:
        when(cond, lambda make=make: make().wait_send())


def compute_steps(R, n, lw, T, W, g_ref, pat_ref, out_ref, a_ref, p_ref, m_ref, acc_ref):
    r = lax.axis_index("row")
    S = 2 * T
    half = n // 2
    M = n * T
    NL = SLOTS * half - 2
    factor = 1.0 / math.sqrt((2 * W - 1) * T)
    scale = factor * factor
    mid = W // 2

    def up(L, e, a):
        return g_ref[L + 1, e // lw, a, (e % lw) * T:(e % lw + 1) * T, :]

    def mask_row(L, e, a):
        return g_ref[L + 1, e // lw, a, lw * T:lw * T + 16, :].astype(jnp.float32)[e % lw:e % lw + 1, :]

    zero = jnp.zeros((T, T), jnp.bfloat16)

    def clear():
        @pl.loop(0, NL + 2 * PAD)
        def _(L):
            a_ref[L] = jnp.zeros((M, S), jnp.bfloat16)
            m_ref[L] = jnp.zeros((n, 8, S), jnp.float32)

        for pad in range(PAD):
            p_ref[pad] = jnp.zeros((M, S), jnp.bfloat16)
            p_ref[NL + PAD + pad] = jnp.zeros((M, S), jnp.bfloat16)

    def left_panel():
        @pl.loop(0, half)
        def _(I):
            for a in range(2):
                i = pl.multiple_of((2 * I + a) * T, T)
                for e in range(W):
                    col, b = (a + e) // 2, (a + e) % 2
                    a_ref[PAD + mid + I + col, pl.ds(i, T), b * T:(b + 1) * T] = up(mid + I, e, a)
                    m_ref[PAD + mid + I + col, 2 * I + a, 0:1, b * T:(b + 1) * T] = mask_row(mid + I, e, a)
                for e in range(1, W):
                    back, b = (a - e) // 2, (a - e) % 2
                    a_ref[PAD + mid + I + back, pl.ds(i, T), b * T:(b + 1) * T] = up(mid + I + back, e, b).T
                    m_ref[PAD + mid + I + back, 2 * I + a, 0:1, b * T:(b + 1) * T] = mask_row(mid + I + back, e, b)

    def super_tile(L, D):
        e = 2 * D
        if D == W // 2:
            top = jnp.concatenate([zero, zero], axis=1)
            low = jnp.concatenate([up(L, W - 1, 1), zero], axis=1)
        else:
            top = jnp.concatenate([up(L, e, 0), up(L, e + 1, 0)], axis=1)
            low = jnp.concatenate([up(L, e - 1, 1), up(L, e, 1)], axis=1)
        return jnp.concatenate([top, low], axis=0)

    def column(src, K, lo, hi):
        def left(*places):
            parts = [src[place, lo:hi, :] for place in places]
            return parts[0] if len(parts) == 1 else jnp.concatenate(parts, axis=1)

        def mirrored(*distances):
            parts = [super_tile(K, D) for D in distances]
            right = parts[0] if len(parts) == 1 else jnp.concatenate(parts, axis=1)
            acc_ref[lo:hi] += lax.dot_general(
                left(*[K + PAD + D for D in distances]), right, (((1,), (1,)), ((), ())),
                preferred_element_type=jnp.float32)

        mirror = up(K, 1, 0)
        diag = jnp.concatenate(
            [jnp.concatenate([up(K, 0, 0), mirror], axis=1),
             jnp.concatenate([mirror.T, up(K, 0, 1)], axis=1)], axis=0)
        acc_ref[lo:hi] = jnp.dot(left(K + PAD), diag, preferred_element_type=jnp.float32)
        for q in range(W // 2 // GROUP):
            steps = [q * GROUP + D for D in range(1, GROUP + 1)]

            @pl.when(K - steps[0] >= 0)
            def _():
                right = jnp.concatenate(
                    [super_tile(jnp.maximum(K - D, 0), D) for D in steps], axis=0)
                acc_ref[lo:hi] += jnp.dot(
                    left(*[K + PAD - D for D in steps]), right, preferred_element_type=jnp.float32)

            @pl.when(K + steps[-1] < NL)
            def _():
                mirrored(*steps)

            for D in steps[:-1]:
                @pl.when((K + D < NL) & (K + steps[-1] >= NL))
                def _(D=D):
                    mirrored(D)

    def square_columns(begin, end):
        @pl.loop(begin, end)
        def _(K):
            column(a_ref, K, 0, M)
            for i in range(n):
                keep = m_ref[K + PAD, i, 0:1, :] * scale
                p_ref[K + PAD, i * T:(i + 1) * T, :] = (
                    keep * acc_ref[i * T:(i + 1) * T, :]).astype(jnp.bfloat16)

    def cube():
        start = mid + r * (lw // 2)
        for jj in range((lw + n) // 2):
            low = max(0, 2 * jj - lw + 1) // 2 * 2
            high = min(n, 2 * jj + 2)
            column(p_ref, start + jj, low * T, high * T)
            for b in range(2):
                for i in range(n):
                    t = 2 * jj + b - i
                    if 0 <= t < lw:
                        total = acc_ref[i * T:(i + 1) * T, b * T:(b + 1) * T]
                        own = g_ref[3 * half + i // 2, r, i % 2, t * T:(t + 1) * T, :].astype(jnp.float32)
                        keep = pat_ref[i, t].astype(jnp.float32) * 0.5
                        out_ref[i, t] = (keep * (3.0 * own - total)).astype(jnp.bfloat16)

    return clear, left_panel, square_columns, cube


def on_device(R, C, matrix_band, pattern, filter_mask):
    n, lw, T, half = plan(matrix_band)
    W = lw * R
    rs = lw * T + 16
    bf = jnp.bfloat16
    NL = SLOTS * half - 2
    return pl.pallas_call(
        functools.partial(kernel, R, C, n, lw, T, W),
        out_shape=jax.ShapeDtypeStruct(matrix_band.shape, bf),
        in_specs=[
            pl.BlockSpec(memory_space=pltpu.VMEM),
            pl.BlockSpec(memory_space=pltpu.SMEM),
            pl.BlockSpec(memory_space=pltpu.SMEM),
        ],
        out_specs=pl.BlockSpec(memory_space=pltpu.VMEM),
        scratch_shapes=[
            pltpu.VMEM((SLOTS * half, R, 2, rs, T), bf),
            pltpu.VMEM((half, 2, rs, T), bf),
            pltpu.VMEM((NL + 2 * PAD, n * T, 2 * T), bf),
            pltpu.VMEM((NL + 2 * PAD, n * T, 2 * T), bf),
            pltpu.VMEM((NL + 2 * PAD, n, 8, 2 * T), jnp.float32),
            pltpu.VMEM((n * T, 2 * T), jnp.float32),
            pltpu.SemaphoreType.DMA((half,)),
            pltpu.SemaphoreType.DMA((SLOTS * half, R)),
            pltpu.SemaphoreType.DMA((3, half)),
            pltpu.SemaphoreType.DMA((4, half, R - 1)),
            pltpu.SemaphoreType.DMA((3, half, R)),
        ],
        compiler_params=pltpu.CompilerParams(
            collective_id=0, has_side_effects=True, vmem_limit_bytes=58 * 2**20),
    )(matrix_band, pattern, filter_mask)


def solution(mesh):
    placed = (P("col", "row", None, None), P("col", "row"), P("col", "row"))
    return jax.shard_map(
        functools.partial(on_device, mesh.shape["row"], mesh.shape["col"]),
        mesh=mesh,
        in_specs=placed,
        out_specs=P("col", "row", None, None),
        check_vma=False,
    )
```

```python
import functools
import math

import jax
import jax.numpy as jnp
from jax import lax
from jax.experimental import pallas as pl
from jax.experimental.pallas import tpu as pltpu
from jax.sharding import PartitionSpec as P

MESH = pl.DeviceIdType.MESH
SLOTS = 7
GROUP = 4
PAD = GROUP - 1


def plan(matrix_band):
    rows, width, tile = matrix_band.shape[0], matrix_band.shape[1], matrix_band.shape[2]
    return rows, width, tile, rows // 2


def kernel(R, C, n, lw, T, W, band_ref, pat_ref, fm_ref, out_ref, g_ref, x_ref, a_ref, p_ref, m_ref, acc_ref,
           local_sem, recv, zsend, rsend, ssend):
    clear, left_panel, square_columns, cube = compute_steps(
        R, n, lw, T, W, g_ref, pat_ref, out_ref, a_ref, p_ref, m_ref, acc_ref)
    r = lax.axis_index("row")
    c = lax.axis_index("col")
    core = lax.rem(c, 2)
    half = n // 2
    sib = c + 1 - 2 * core
    right, left = lax.rem(c + 2, C), lax.rem(c + C - 2, C)
    third = lax.rem(c + C - 3 + 6 * core, C)
    if R == 4:
        side, over = r + 1 - 2 * lax.rem(r, 2), lax.rem(r + 2, 4)
        near, others = [side, over], [side, over, lax.rem(side + 2, 4)]
    else:
        others = near = [lax.rem(r + d, R) for d in range(1, R)]

    barrier = pltpu.get_barrier_semaphore()
    partners = [(r, sib), (r, right), (r, left), (r, third)] + [(o, c) for o in near]
    for p in partners:
        pl.semaphore_signal(barrier, inc=1, device_id=p, device_id_type=MESH)

    for h in range(half):
        for a in range(2):
            i = 2 * h + a
            for t in range(lw):
                m = pat_ref[i, t].astype(jnp.float32)
                tile = band_ref[i, t].astype(jnp.float32) * m
                x_ref[h, a, t * T:(t + 1) * T, :] = tile.astype(jnp.bfloat16)
            pos = lax.broadcasted_iota(jnp.int32, (16, 128), 0)
            mask = jnp.zeros((16, 128), jnp.float32)
            for t in range(lw):
                mask = jnp.where(pos == t, fm_ref[i, t].astype(jnp.float32), mask)
            x_ref[h, a, lw * T:lw * T + 16, :] = mask.astype(jnp.bfloat16)

    pl.semaphore_wait(barrier, len(partners))

    def remote(src, g, rr, send_sem, dev):
        return pltpu.make_async_remote_copy(
            src_ref=src, dst_ref=g_ref.at[g, rr], send_sem=send_sem,
            recv_sem=recv.at[g, rr], device_id=dev, device_id_type=MESH)

    def when(cond, fn):
        if cond is True:
            fn()
        else:
            pl.when(cond)(fn)

    def arrived(g, rr):
        pltpu.make_async_copy(g_ref.at[g, rr], g_ref.at[g, rr], recv.at[g, rr]).wait()

    def g5(h, rr):
        return 2 * h + rr * lw <= 15 - 6 * core

    def g6(h, rr):
        return 2 * h + rr * lw <= 3

    own = lambda h: x_ref.at[h]
    sends = []

    def start(cond, make, waiters):
        when(cond, lambda: make().start())
        sends.append((cond, make))

    for h in range(half):
        start(True, lambda h=h: remote(own(h), half + h, r, zsend.at[0, h], (r, right)), sends)
        start(g5(h, r), lambda h=h: remote(own(h), 5 * half + h, r, zsend.at[1, h], (r, left)), sends)
    for h in range(half):
        if h >= 1:
            start(core == 1, lambda h=h: remote(own(h), h, r, zsend.at[2, h], (r, third)), sends)
        if h <= 1:
            start((core == 0) & g6(h, r),
                  lambda h=h: remote(own(h), 6 * half + h, r, zsend.at[2, h], (r, third)), sends)
    for h in range(half):
        for d, o in enumerate(near):
            start(True, lambda h=h, d=d, o=o: remote(own(h), 3 * half + h, r, rsend.at[3, h, d], (o, c)), sends)
        start(True, lambda h=h: remote(own(h), (4 * core + 2 * (1 - core)) * half + h, r,
                                       ssend.at[1, h, r], (r, sib)), sends)
        pltpu.make_async_copy(own(h), g_ref.at[3 * half + h, r], local_sem.at[h]).start()

    def to_row(cond, q, g, h):
        for d, o in enumerate(near):
            start(cond, lambda d=d, o=o: remote(g_ref.at[g, r], g, r, rsend.at[q, h, d], (o, c)), sends)

    def to_sib(q, s, h, rr):
        g = s * half + h
        dst = (s - 1 + 2 * core) * half + h
        if s == 1:
            cond = True if h >= 1 else core == 1
        elif s == 3:
            cond = True
        else:
            low = (core == 0) & (2 * h + rr * lw <= 15)
            cond = low | ((core == 1) & (2 * h + rr * lw <= 3)) if h <= 1 else low
        start(cond, lambda: remote(g_ref.at[g, rr], dst, rr, ssend.at[q, h, rr], (r, sib)), sends)

    def to_diagonal(cond, q, s, h, index):
        if R != 4 or index != (s // 2 + h) % 2:
            return
        g, rr, dev = s * half + h, near[index], (near[1 - index], c)
        start(cond, lambda: remote(g_ref.at[g, rr], g, rr, rsend.at[q, h, 2], dev), sends)

    clear()

    for h in range(half):
        arrived(half + h, r)
        to_row(True, 0, half + h, h)
        to_sib(0, 1, h, r)
        for d, o in enumerate(others):
            arrived(3 * half + h, o)
            to_diagonal(True, 3, 3, h, d)
            to_sib(1, 3, h, o)
    for h in range(half):
        if h >= 1:
            when(core == 0, lambda h=h: arrived(h, r))
            to_row(core == 0, 2, h, h)
        if h <= 1:
            cond = (core == 1) & g6(h, r)
            when(cond, lambda h=h: arrived(6 * half + h, r))
            to_row(cond, 2, 6 * half + h, h)
    for h in range(half):
        when(g5(h, r), lambda h=h: arrived(5 * half + h, r))
        to_row(g5(h, r), 1, 5 * half + h, h)
        to_sib(2, 5, h, r)
    for h in range(half):
        for d, o in enumerate(others):
            arrived(half + h, o)
            to_diagonal(True, 0, 1, h, d)
            to_sib(0, 1, h, o)
    for h in range(half):
        for d, o in enumerate(others):
            if h >= 1:
                when(core == 0, lambda h=h, o=o: arrived(h, o))
                to_diagonal(core == 0, 2, 0, h, d)
            if h <= 1:
                cond = (core == 1) & g6(h, o)
                when(cond, lambda h=h, o=o: arrived(6 * half + h, o))
                to_diagonal(cond, 2, 6, h, d)
    for h in range(half):
        for rr in range(R):
            arrived(2 * half + h, rr)
            if h >= 1:
                when(core == 1, lambda h=h, rr=rr: arrived(h, rr))
        pltpu.make_async_copy(own(h), g_ref.at[3 * half + h, r], local_sem.at[h]).wait()
    left_panel()
    first = 4 * half - 1
    for h in range(half):
        for d, o in enumerate(others):
            when(g5(h, o), lambda h=h, o=o: arrived(5 * half + h, o))
            to_diagonal(g5(h, o), 1, 5, h, d)
            to_sib(2, 5, h, o)
        square_columns(h * first // half, (h + 1) * first // half)
    for h in range(half):
        for rr in range(R):
            when((core == 0) | (2 * h + rr * lw <= 15), lambda h=h, rr=rr: arrived(4 * half + h, rr))
            if h <= 1 and 2 * h + rr * lw <= 3:
                when(core == 0, lambda h=h, rr=rr: arrived(6 * half + h, rr))
    square_columns(first, SLOTS * half - 2)
    cube()
    for cond, make in sends:
        when(cond, lambda make=make: make().wait_send())


def compute_steps(R, n, lw, T, W, g_ref, pat_ref, out_ref, a_ref, p_ref, m_ref, acc_ref):
    r = lax.axis_index("row")
    S = 2 * T
    half = n // 2
    M = n * T
    NL = SLOTS * half - 2
    factor = 1.0 / math.sqrt((2 * W - 1) * T)
    scale = factor * factor
    mid = W // 2

    def up(L, e, a):
        return g_ref[L + 1, e // lw, a, (e % lw) * T:(e % lw + 1) * T, :]

    def mask_row(L, e, a):
        return g_ref[L + 1, e // lw, a, lw * T:lw * T + 16, :].astype(jnp.float32)[e % lw:e % lw + 1, :]

    zero = jnp.zeros((T, T), jnp.bfloat16)

    def clear():
        @pl.loop(0, NL + 2 * PAD)
        def _(L):
            a_ref[L] = jnp.zeros((M, S), jnp.bfloat16)
            m_ref[L] = jnp.zeros((n, 8, S), jnp.float32)

        for pad in range(PAD):
            p_ref[pad] = jnp.zeros((M, S), jnp.bfloat16)
            p_ref[NL + PAD + pad] = jnp.zeros((M, S), jnp.bfloat16)

    def left_panel():
        @pl.loop(0, half)
        def _(I):
            for a in range(2):
                i = pl.multiple_of((2 * I + a) * T, T)
                for e in range(W):
                    col, b = (a + e) // 2, (a + e) % 2
                    a_ref[PAD + mid + I + col, pl.ds(i, T), b * T:(b + 1) * T] = up(mid + I, e, a)
                    m_ref[PAD + mid + I + col, 2 * I + a, 0:1, b * T:(b + 1) * T] = mask_row(mid + I, e, a)
                for e in range(1, W):
                    back, b = (a - e) // 2, (a - e) % 2
                    a_ref[PAD + mid + I + back, pl.ds(i, T), b * T:(b + 1) * T] = up(mid + I + back, e, b).T
                    m_ref[PAD + mid + I + back, 2 * I + a, 0:1, b * T:(b + 1) * T] = mask_row(mid + I + back, e, b)

    def super_tile(L, D):
        e = 2 * D
        if D == W // 2:
            top = jnp.concatenate([zero, zero], axis=1)
            low = jnp.concatenate([up(L, W - 1, 1), zero], axis=1)
        else:
            top = jnp.concatenate([up(L, e, 0), up(L, e + 1, 0)], axis=1)
            low = jnp.concatenate([up(L, e - 1, 1), up(L, e, 1)], axis=1)
        return jnp.concatenate([top, low], axis=0)

    def column(src, K, lo, hi):
        def left(*places):
            parts = [src[place, lo:hi, :] for place in places]
            return parts[0] if len(parts) == 1 else jnp.concatenate(parts, axis=1)

        def mirrored(*distances):
            parts = [super_tile(K, D) for D in distances]
            right = parts[0] if len(parts) == 1 else jnp.concatenate(parts, axis=1)
            acc_ref[lo:hi] += lax.dot_general(
                left(*[K + PAD + D for D in distances]), right, (((1,), (1,)), ((), ())),
                preferred_element_type=jnp.float32)

        mirror = up(K, 1, 0)
        diag = jnp.concatenate(
            [jnp.concatenate([up(K, 0, 0), mirror], axis=1),
             jnp.concatenate([mirror.T, up(K, 0, 1)], axis=1)], axis=0)
        acc_ref[lo:hi] = jnp.dot(left(K + PAD), diag, preferred_element_type=jnp.float32)
        for q in range(W // 2 // GROUP):
            steps = [q * GROUP + D for D in range(1, GROUP + 1)]

            @pl.when(K - steps[0] >= 0)
            def _():
                right = jnp.concatenate(
                    [super_tile(jnp.maximum(K - D, 0), D) for D in steps], axis=0)
                acc_ref[lo:hi] += jnp.dot(
                    left(*[K + PAD - D for D in steps]), right, preferred_element_type=jnp.float32)

            @pl.when(K + steps[-1] < NL)
            def _():
                mirrored(*steps)

            for D in steps[:-1]:
                @pl.when((K + D < NL) & (K + steps[-1] >= NL))
                def _(D=D):
                    mirrored(D)

    def square_columns(begin, end):
        @pl.loop(begin, end)
        def _(K):
            column(a_ref, K, 0, M)
            for i in range(n):
                keep = m_ref[K + PAD, i, 0:1, :] * scale
                p_ref[K + PAD, i * T:(i + 1) * T, :] = (
                    keep * acc_ref[i * T:(i + 1) * T, :]).astype(jnp.bfloat16)

    def cube():
        start = mid + r * (lw // 2)
        for jj in range((lw + n) // 2):
            low = max(0, 2 * jj - lw + 1) // 2 * 2
            high = min(n, 2 * jj + 2)
            column(p_ref, start + jj, low * T, high * T)
            for b in range(2):
                for i in range(n):
                    t = 2 * jj + b - i
                    if 0 <= t < lw:
                        total = acc_ref[i * T:(i + 1) * T, b * T:(b + 1) * T]
                        own = g_ref[3 * half + i // 2, r, i % 2, t * T:(t + 1) * T, :].astype(jnp.float32)
                        keep = pat_ref[i, t].astype(jnp.float32) * 0.5
                        out_ref[i, t] = (keep * (3.0 * own - total)).astype(jnp.bfloat16)

    return clear, left_panel, square_columns, cube


def on_device(R, C, matrix_band, pattern, filter_mask):
    n, lw, T, half = plan(matrix_band)
    W = lw * R
    rs = lw * T + 16
    bf = jnp.bfloat16
    NL = SLOTS * half - 2
    return pl.pallas_call(
        functools.partial(kernel, R, C, n, lw, T, W),
        out_shape=jax.ShapeDtypeStruct(matrix_band.shape, bf),
        in_specs=[
            pl.BlockSpec(memory_space=pltpu.VMEM),
            pl.BlockSpec(memory_space=pltpu.SMEM),
            pl.BlockSpec(memory_space=pltpu.SMEM),
        ],
        out_specs=pl.BlockSpec(memory_space=pltpu.VMEM),
        scratch_shapes=[
            pltpu.VMEM((SLOTS * half, R, 2, rs, T), bf),
            pltpu.VMEM((half, 2, rs, T), bf),
            pltpu.VMEM((NL + 2 * PAD, n * T, 2 * T), bf),
            pltpu.VMEM((NL + 2 * PAD, n * T, 2 * T), bf),
            pltpu.VMEM((NL + 2 * PAD, n, 8, 2 * T), jnp.float32),
            pltpu.VMEM((n * T, 2 * T), jnp.float32),
            pltpu.SemaphoreType.DMA((half,)),
            pltpu.SemaphoreType.DMA((SLOTS * half, R)),
            pltpu.SemaphoreType.DMA((3, half)),
            pltpu.SemaphoreType.DMA((4, half, R - 1)),
            pltpu.SemaphoreType.DMA((3, half, R)),
        ],
        compiler_params=pltpu.CompilerParams(
            collective_id=0, has_side_effects=True, vmem_limit_bytes=58 * 2**20),
    )(matrix_band, pattern, filter_mask)


def solution(mesh):
    placed = (P("col", "row", None, None), P("col", "row"), P("col", "row"))
    return jax.shard_map(
        functools.partial(on_device, mesh.shape["row"], mesh.shape["col"]),
        mesh=mesh,
        in_specs=placed,
        out_specs=P("col", "row", None, None),
        check_vma=False,
    )
```
